512 devices in a mesh: tm: 8 (over x, core), seq: 64 (over y, z).
Axes of the slice: x: 4, y: 8, z: 8, core: 2. Of those that a mesh axis runs over, the one named last changes fastest.
Arguments:
- latents: bfloat16 [8, 1024, 4096], P('tm', 'seq'), may hold values from -14 to 14
- end_latent: bfloat16 [1024, 4096], P('seq'), may hold values from -14 to 14
- timesteps: int32 [9], replicated, may hold values from 0 to 1000, as said below
- modulation: float32 [8, 3, 4096], P('tm'), may hold values from -10 to 10
- proj_weight: bfloat16 [3, 32, 128, 128], replicated, may hold values from -1 to 1
Outputs:
- new_latents: bfloat16 [8, 1024, 4096], P('tm', 'seq')
- update_error: float32 [8, 1024], P('tm', 'seq')
The draws below stay inside these ranges and needn't reach their ends.
Inputs may be any that keep to these rules, and one draw needn't show every extreme that they name: `timesteps`: strictly decreasing.
All inputs are finite; a program needn't handle non-finite values.
Results may differ from the reference program's by a relative error of at most 0.0065.
Values may be sent and summed in bfloat16 or wider, within the bound.
No kernel may reach another device: no remote copies, remote signals or barrier semaphores. Data moves between devices by JAX's collectives and lax.ppermute only.
A program may use at most 64 MiB of HBM per device.

```python
import math
import jax
import jax.numpy as jnp
from jax import lax

HEADS = 32
DH = 128
D = 4096
L = 1024
WIN = 8


def shared_start(key):
    key = jax.random.fold_in(key, 7)
    keys = jax.random.split(key, 2)
    scales = jnp.exp(jax.random.uniform(keys[0], (D,), jnp.float32, math.log(0.3), math.log(3.0)))
    start = jnp.clip(jax.random.normal(keys[1], (L, D), jnp.float32), -4.0, 4.0)
    return (start, scales)


def deviation(key, shape):
    field = jnp.clip(jax.random.normal(key, shape, jnp.float32), -4.0, 4.0)
    return field


def draw_latents(key, part):
    start, scales = shared_start(key)
    key = jax.random.fold_in(key, 11)
    spread = 0.6 * jnp.arange(WIN, dtype=jnp.float32) / WIN
    field = start[None] + spread[:, None, None] * scales * deviation(key, (WIN, L, D))
    return jnp.clip(field, -14.0, 14.0).astype(jnp.bfloat16)


def draw_end_latent(key, part):
    start, scales = shared_start(key)
    key = jax.random.fold_in(key, 12)
    field = start + 0.6 * scales * deviation(key, (L, D))
    return jnp.clip(field, -14.0, 14.0).astype(jnp.bfloat16)


def draw_timesteps(key, part):
    key = jax.random.fold_in(key, 13)
    first_key, second_key = jax.random.split(key)
    start = 1000 - jax.random.randint(first_key, (1,), 0, 40)
    strides = jax.random.randint(second_key, (WIN,), 80, 121)
    return jnp.concatenate([start, start - jnp.cumsum(strides)]).astype(jnp.int32)


def draw_modulation(key, part):
    key = jax.random.fold_in(key, 14)
    keys = jax.random.split(key, 4)
    signs = jnp.where(jax.random.randint(keys[3], (WIN, D), 0, 2) == 0, -1.0, 1.0)
    shift = jnp.clip(0.9 * jax.random.normal(keys[0], (WIN, D), jnp.float32), -3.6, 3.6)
    scale = jnp.clip(0.8 * jax.random.normal(keys[1], (WIN, D), jnp.float32), -3.2, 3.2)
    gate = jnp.exp(jax.random.uniform(keys[2], (WIN, D), jnp.float32, 0.0, math.log(10.0)))
    return jnp.stack([shift, scale, signs * gate], axis=1).astype(jnp.float32)


def draw_proj_weight(key, part):
    key = jax.random.fold_in(key, 15)
    width = DH ** (-0.5)
    stacked = jnp.clip(jax.random.normal(key, (3, HEADS, DH, DH), jnp.float32), -4.0, 4.0) * width
    return jnp.clip(stacked, -1.0, 1.0).astype(jnp.bfloat16)


def setup_inputs(seed: int = 0) -> dict:
    splits = jax.random.split(jax.random.key(seed), 6)
    latents = draw_latents(jax.random.fold_in(splits[5], 71), 0)
    end_latent = draw_end_latent(jax.random.fold_in(splits[5], 71), 0)
    timesteps = draw_timesteps(jax.random.fold_in(splits[5], 71), 0)
    modulation = draw_modulation(jax.random.fold_in(splits[5], 71), 0)
    proj_weight = draw_proj_weight(jax.random.fold_in(splits[5], 71), 0)
    return dict(latents=latents, end_latent=end_latent, timesteps=timesteps, modulation=modulation, proj_weight=proj_weight)


def sigmas_of(timesteps):
    frac = timesteps.astype(jnp.float32) / 1000.0
    return 5.0 * frac / (1.0 + 4.0 * frac)

def head_attention(operands):
    query, key_rows, values = operands
    scores = jnp.dot(query, key_rows.T, preferred_element_type=jnp.float32) * (1.0 / math.sqrt(DH))
    row_max = lax.optimization_barrier(jnp.max(scores, axis=-1, keepdims=True))
    probs = jnp.exp(scores - row_max)
    row_total = lax.optimization_barrier(jnp.sum(probs, axis=-1, keepdims=True))
    mixed = jnp.dot(probs.astype(jnp.bfloat16), values, preferred_element_type=jnp.float32) / row_total
    return mixed.astype(jnp.bfloat16)

def evaluate(latent, factors, proj_weight):
    modulated = (latent.astype(jnp.float32) * (1.0 + factors[1]) + factors[0]).astype(jnp.bfloat16)
    split_heads = modulated.reshape(L, HEADS, DH).astype(jnp.float32)
    weights = proj_weight.astype(jnp.float32)
    query = jnp.einsum('lhd,hde->hle', split_heads, weights[0]).astype(jnp.bfloat16)
    key_rows = jnp.einsum('lhd,hde->hle', split_heads, weights[1]).astype(jnp.bfloat16)
    values = jnp.einsum('lhd,hde->hle', split_heads, weights[2]).astype(jnp.bfloat16)
    mixed = lax.map(head_attention, (query, key_rows, values))
    return mixed.transpose(1, 0, 2).reshape(L, D)

def reference(latents, end_latent, timesteps, modulation, proj_weight):
    sigmas = sigmas_of(timesteps)
    step_sizes = sigmas[1:] - sigmas[:-1]
    running = latents[0].astype(jnp.float32)
    results = []
    errors = []
    for step in range(WIN):
        attention = evaluate(latents[step], modulation[step], proj_weight)
        drift = step_sizes[step] * modulation[step, 2] * attention.astype(jnp.float32)
        running = running + drift
        old_next = latents[step + 1] if step + 1 < WIN else end_latent
        errors.append(lax.optimization_barrier(jnp.mean((running - old_next.astype(jnp.float32)) ** 2, axis=-1)))
        results.append(running.astype(jnp.bfloat16))
    return (jnp.stack(results), jnp.stack(errors))
```

```python
import math

import jax
import jax.numpy as jnp
from jax import lax
from jax.sharding import Mesh, PartitionSpec as P


def sigmas_of(timesteps):
    frac = timesteps.astype(jnp.float32) / 1000.0
    return 5.0 * frac / (1.0 + 4.0 * frac)


def attend(tokens, factors, weights, half):
    sources, rows, size = tokens.shape
    modulated = (tokens.astype(jnp.float32) * (1.0 + factors[1]) + factors[0]).astype(jnp.bfloat16)
    halves = modulated.reshape(sources, 2, rows // 2, size)
    own = jnp.where(half == 0, halves[:, 0], halves[:, 1]).reshape(sources * rows // 2, size)
    every = modulated.reshape(sources * rows, size)

    def project(block, weight):
        return jnp.dot(block, weight, preferred_element_type=jnp.float32).astype(jnp.bfloat16)

    query = project(own, weights[0])
    key = project(every, weights[1])
    value = project(every, weights[2])
    scores = lax.dot_general(
        query, key, (((1,), (1,)), ((), ())), preferred_element_type=jnp.float32
    ) * (1.0 / math.sqrt(size))
    probs = jnp.exp(scores - jnp.max(scores, axis=-1, keepdims=True))
    total = jnp.sum(probs, axis=-1, keepdims=True)
    mixed = jnp.dot(probs.astype(jnp.bfloat16), value, preferred_element_type=jnp.float32) / total
    return mixed.astype(jnp.bfloat16).reshape(sources, rows // 2, size)


def body(latents, end_latent, timesteps, modulation, proj_weight):
    heads, size = proj_weight.shape[1], proj_weight.shape[2]
    rows, width = latents.shape[1:]
    across, cores, group = lax.axis_size("x"), lax.axis_size("core"), lax.axis_size("seq")
    own_x, own_core, place = lax.axis_index("x"), lax.axis_index("core"), lax.axis_index("seq")
    time_index = own_x * cores + own_core
    copies = group // heads
    head, half = place // copies, place % copies
    own_latent = latents[0]

    window = lax.all_gather(own_latent, ("x", "core"))

    blocks = own_latent.reshape(rows, heads, size).transpose(1, 0, 2)
    sent = jnp.repeat(blocks, copies, axis=0)
    tokens = lax.all_to_all(sent, "seq", 0, 0, tiled=True)
    factors = lax.dynamic_index_in_dim(modulation[0].reshape(3, heads, size), head, 1, False)
    weights = lax.dynamic_index_in_dim(proj_weight, head, 1, False)
    mixed = attend(tokens, factors, weights, half)
    returned = lax.all_to_all(mixed, "seq", 0, 0, tiled=True)
    attention = returned.reshape(heads, copies, rows // copies, size).transpose(1, 2, 0, 3)
    attention = attention.reshape(rows, width).astype(jnp.float32)

    sigmas = sigmas_of(timesteps)
    pair = lax.dynamic_slice_in_dim(sigmas, time_index, 2)
    drift = (pair[1] - pair[0]) * modulation[0, 2] * attention
    spread = jnp.broadcast_to(drift.astype(jnp.bfloat16)[None], (across, rows, width))
    along = lax.all_to_all(spread, "x", 0, 0, tiled=True)
    before = (jnp.arange(across) < own_x)[:, None, None]
    earlier = jnp.sum(jnp.where(before, along.astype(jnp.float32), 0.0), axis=0)
    upto = earlier + drift
    pairs = lax.all_gather(jnp.where(own_core == 0, upto, earlier), "core")
    updated = window[0].astype(jnp.float32) + upto + jnp.where(own_core == 0, pairs[1], pairs[0])
    last = time_index == across * cores - 1
    ahead = lax.dynamic_index_in_dim(window, jnp.where(last, 0, time_index + 1), 0, False)
    old = jnp.where(last, end_latent, ahead).astype(jnp.float32)
    error = jnp.mean((updated - old) ** 2, axis=-1)
    return (updated.astype(jnp.bfloat16)[None], error[None])


def solution(mesh):
    inner = Mesh(mesh.devices.reshape(-1, 2, mesh.shape["seq"]), ("x", "core", "seq"))
    time = ("x", "core")
    return jax.shard_map(
        body,
        mesh=inner,
        in_specs=(P(time, "seq", None), P("seq", None), P(), P(time, None, None), P()),
        out_specs=(P(time, "seq", None), P(time, "seq")),
        check_vma=False,
    )
```

```python
import functools
import math

import jax
import jax.numpy as jnp
from jax import lax
from jax.experimental import pallas as pl
from jax.experimental.pallas import tpu as pltpu
from jax.sharding import Mesh, PartitionSpec as P

VMEM = pl.BlockSpec(memory_space=pltpu.VMEM)
HBM = pl.BlockSpec(memory_space=pltpu.HBM)


def call(kernel, shapes, *operands, specs=None, scratch=(), limit=32 << 20):
    return pl.pallas_call(
        kernel,
        out_shape=shapes,
        in_specs=[VMEM] * len(operands) if specs is None else specs,
        out_specs=jax.tree.map(lambda _: VMEM, shapes),
        scratch_shapes=scratch,
        compiler_params=pltpu.CompilerParams(vmem_limit_bytes=limit),
    )(*operands)


def own_head(heads):
    return lax.rem(lax.axis_index("near"), heads)


def cut_kernel(
    latent_hbm, modulation_hbm, weights_hbm, sent_ref, own_ref, modulation_ref, weights_ref, *done
):
    size = sent_ref.shape[2]
    heads = weights_hbm.shape[1]
    copies = sent_ref.shape[0] // heads
    fetches = [
        pltpu.make_async_copy(latent_hbm, own_ref, done[0]),
        pltpu.make_async_copy(modulation_hbm, modulation_ref, done[1]),
        pltpu.make_async_copy(weights_hbm.at[:, own_head(heads)], weights_ref, done[2]),
    ]
    for fetch in fetches:
        fetch.start()
    fetches[0].wait()
    for head in range(heads):
        block = own_ref[:, head * size : (head + 1) * size]
        for copy in range(copies):
            sent_ref[copy * heads + head] = block
    fetches[1].wait()
    fetches[2].wait()


def attend_kernel(chunk, heads, tokens_ref, modulation_ref, weights_ref, mixed_ref):
    total_rows, size = tokens_ref.shape
    queries = mixed_ref.shape[0]
    columns = pl.ds(pl.multiple_of(own_head(heads) * size, size), size)
    shift, scale = modulation_ref[0, :, columns], modulation_ref[1, :, columns]

    def modulate(block):
        return (block.astype(jnp.float32) * (1.0 + scale) + shift).astype(jnp.bfloat16)

    def project(block, which):
        product = jnp.dot(block, weights_ref[which], preferred_element_type=jnp.float32)
        return product.astype(jnp.bfloat16)

    every = modulate(tokens_ref[...])
    start = pl.multiple_of(lax.axis_index("far") * queries, queries)
    query = project(modulate(tokens_ref[pl.ds(start, queries), :]), 0)
    key, value = project(every, 1), project(every, 2)
    factor = math.log2(math.e) / math.sqrt(size)
    for start in range(0, queries, chunk):
        scores = lax.dot_general(
            query[start : start + chunk],
            key,
            (((1,), (1,)), ((), ())),
            preferred_element_type=jnp.float32,
        )
        row_max = jnp.max(scores, axis=-1, keepdims=True)
        probs = jnp.exp2(scores * factor - row_max * factor)
        total = jnp.sum(probs, axis=-1, keepdims=True)
        mixed = jnp.dot(probs.astype(jnp.bfloat16), value, preferred_element_type=jnp.float32)
        mixed_ref[start : start + chunk, :] = (mixed / total).astype(jnp.bfloat16)


def spread_kernel(times_ref, modulation_ref, back_ref, own_ref, drift_ref, sent_ref):
    heads, _, size = back_ref.shape
    across = sent_ref.shape[0]
    own_x = lax.axis_index("x")
    time = own_x * lax.axis_size("core") + lax.axis_index("core")
    times = times_ref[...].astype(jnp.float32) / 1000.0
    sigmas = 5.0 * times / (1.0 + 4.0 * times)
    points = lax.broadcasted_iota(jnp.int32, sigmas.shape, 1)
    signed = jnp.where(points == time + 1, sigmas, jnp.where(points == time, -sigmas, 0.0))
    step = jnp.sum(signed, axis=-1, keepdims=True)
    for head in range(heads):
        columns = slice(head * size, (head + 1) * size)
        own = own_ref[:, columns]
        drift = (step * modulation_ref[2, :, columns]) * back_ref[head].astype(jnp.float32)
        drift = drift + jnp.where(time == 0, own.astype(jnp.float32), 0.0)
        drift_ref[:, columns] = drift
        low = drift.astype(jnp.bfloat16)
        for target in range(across):
            sent_ref[target, :, columns] = jnp.where(target > own_x, low, own)


def gather_kernel(own_ref, drift_ref, along_ref, upto_ref, given_ref):
    across, rows, width = along_ref.shape
    own_x, odd = lax.axis_index("x"), lax.axis_index("core") == 1
    later = jnp.minimum(own_x + 1, across - 1)
    for start in range(0, width, 512):
        columns = slice(start, start + 512)
        earlier = jnp.zeros((rows, 512), jnp.float32)
        for source in range(across - 1):
            term = along_ref[source, :, columns].astype(jnp.float32)
            earlier = earlier + jnp.where(source < own_x, term, 0.0)
        upto = earlier + drift_ref[:, columns]
        upto_ref[:, columns] = upto
        given_ref[:rows, columns] = jnp.where(odd, earlier, upto).astype(jnp.bfloat16)
        given_ref[rows:, columns] = jnp.where(odd, own_ref[:, columns], along_ref[later, :, columns])


def finish_kernel(upto_ref, pairs_ref, end_ref, new_ref, error_ref):
    rows, width = upto_ref.shape
    odd = lax.axis_index("core") == 1
    last = jnp.logical_and(odd, lax.axis_index("x") == lax.axis_size("x") - 1)
    squares = jnp.zeros((rows, 128), jnp.float32)
    for start in range(0, width, 512):
        columns = slice(start, start + 512)
        other = jnp.where(odd, pairs_ref[0, :, columns], pairs_ref[1, :, columns])
        updated = upto_ref[:, columns] + other[:rows].astype(jnp.float32)
        new_ref[:, columns] = updated.astype(jnp.bfloat16)
        old = jnp.where(last, end_ref[:, columns], other[rows:])
        change = updated - old.astype(jnp.float32)
        change = change * change
        for part in range(0, 512, 128):
            squares = squares + change[:, part : part + 128]
    error_ref[...] = jnp.sum(squares.T, axis=0, keepdims=True) * (1.0 / width)


def body(latents, end_latent, timesteps, modulation, proj_weight):
    heads, size = proj_weight.shape[1], proj_weight.shape[2]
    rows, width = latents.shape[1:]
    across, group = lax.axis_size("x"), lax.axis_size("far") * lax.axis_size("near")
    copies = group // heads

    def low(*shape):
        return jax.ShapeDtypeStruct(shape, jnp.bfloat16)

    def wide(*shape):
        return jax.ShapeDtypeStruct(shape, jnp.float32)

    sent, own_latent, modulation, weights = call(
        cut_kernel,
        [low(group, rows, size), low(rows, width), wide(3, 1, width), low(3, size, size)],
        *(
            pltpu.with_memory_space_constraint(operand, pltpu.HBM)
            for operand in (latents[0], modulation.transpose(1, 0, 2), proj_weight)
        ),
        specs=[HBM] * 3,
        scratch=[pltpu.SemaphoreType.DMA] * 3,
    )
    tokens = lax.all_to_all(sent, ("far", "near"), 0, 0, tiled=True).reshape(group * rows, size)
    mixed = call(
        functools.partial(attend_kernel, 128, heads),
        low(group * rows // copies, size),
        tokens,
        modulation,
        weights,
    ).reshape(heads, rows, size)
    back = lax.all_to_all(mixed, "near", 0, 0, tiled=True)
    drift, along = call(
        spread_kernel,
        [wide(rows, width), low(across, rows, width)],
        timesteps.reshape(1, -1),
        modulation,
        back,
        own_latent,
    )
    along = lax.all_to_all(along, "x", 0, 0, tiled=True)
    upto, given = call(
        gather_kernel, [wide(rows, width), low(2 * rows, width)], own_latent, drift, along
    )
    pairs = lax.all_gather(given, "core")
    new, error = call(finish_kernel, [low(rows, width), wide(1, rows)], upto, pairs, end_latent)
    return (new[None], error)


def solution(mesh):
    inner = Mesh(
        mesh.devices.reshape(-1, 2, mesh.shape["seq"] // 32, 32), ("x", "core", "far", "near")
    )
    time, seq = ("x", "core"), ("far", "near")
    return jax.shard_map(
        body,
        mesh=inner,
        in_specs=(P(time, seq, None), P(seq, None), P(), P(time, None, None), P()),
        out_specs=(P(time, seq, None), P(time, seq)),
        check_vma=False,
    )
```

```python
import functools
import math

import jax
import jax.numpy as jnp
from jax import lax
from jax.experimental import pallas as pl
from jax.experimental.pallas import tpu as pltpu
from jax.sharding import Mesh, PartitionSpec as P

VMEM = pl.BlockSpec(memory_space=pltpu.VMEM)
HBM = pl.BlockSpec(memory_space=pltpu.HBM)


def call(kernel, shapes, *operands, specs=None, scratch=()):
    return pl.pallas_call(
        kernel,
        out_shape=shapes,
        in_specs=[VMEM] * len(operands) if specs is None else specs,
        out_specs=jax.tree.map(lambda _: VMEM, shapes),
        scratch_shapes=scratch,
        compiler_params=pltpu.CompilerParams(vmem_limit_bytes=32 << 20),
    )(*operands)


BITS = ("y2", "y1", "y0", "z2", "z1", "z0")
ORDER = ('y0', 'y1', 'y2', 'z2', 'z1', 'z0')
FAR = "z2"
NEAR = tuple(axis for axis in ORDER if axis != FAR)
ACROSS = ("x1", "x0")
AFTER = 1 << (len(ORDER) - 1 - ORDER.index(FAR))


def step_size(times_ref, time):
    times = times_ref[...].astype(jnp.float32) / 1000.0
    sigmas = 5.0 * times / (1.0 + 4.0 * times)
    points = lax.broadcasted_iota(jnp.int32, sigmas.shape, 1)
    signed = jnp.where(points == time + 1, sigmas, jnp.where(points == time, -sigmas, 0.0))
    return jnp.sum(signed, axis=-1, keepdims=True)


def own_time():
    return lax.axis_index(ACROSS) * lax.axis_size("core") + lax.axis_index("core")


def cut_kernel(
    latent_hbm, weights_hbm, modulation_hbm, times_hbm, end_hbm,
    sent_ref, own_ref, weights_ref, modulation_ref, times_ref, end_ref,
    *done,
):
    before, copies, after, _, size = sent_ref.shape
    fetches = [
        pltpu.make_async_copy(source, target, semaphore)
        for source, target, semaphore in (
            (latent_hbm, own_ref, done[0]),
            (weights_hbm.at[:, lax.axis_index(NEAR)], weights_ref, done[1]),
            (modulation_hbm, modulation_ref, done[2]),
            (times_hbm, times_ref, done[3]),
            (end_hbm, end_ref, done[4]),
        )
    ]
    for fetch in fetches:
        fetch.start()
    fetches[0].wait()
    for head in range(before * after):
        block = own_ref[:, head * size : (head + 1) * size]
        for copy in range(copies):
            sent_ref[head // after, copy, head % after] = block
    for fetch in fetches[1:]:
        fetch.wait()


def attend_kernel(chunk, tokens_ref, times_ref, modulation_ref, weights_ref, sent_ref):
    across, queries, size = sent_ref.shape
    columns = pl.ds(pl.multiple_of(lax.axis_index(NEAR) * size, size), size)
    own_x, time = lax.axis_index(ACROSS), own_time()
    shift, scale = modulation_ref[0, :, columns], modulation_ref[1, :, columns]
    rate = step_size(times_ref, time) * modulation_ref[2, :, columns]

    def modulate(block):
        return (block.astype(jnp.float32) * (1.0 + scale) + shift).astype(jnp.bfloat16)

    def project(block, which):
        product = jnp.dot(block, weights_ref[which], preferred_element_type=jnp.float32)
        return product.astype(jnp.bfloat16)

    every = modulate(tokens_ref[...].reshape(2 * queries, size))
    latent = tokens_ref[:, lax.axis_index(FAR)].reshape(queries, size)
    query, key, value = project(modulate(latent), 0), project(every, 1), project(every, 2)
    factor = math.log2(math.e) / math.sqrt(size)

    def score(start):
        block = query[start : start + chunk]
        return lax.dot_general(
            block, key, (((1,), (1,)), ((), ())), preferred_element_type=jnp.float32
        )

    following = score(0)
    for start in range(0, queries, chunk):
        scores = following
        if start + chunk < queries:
            following = score(start + chunk)
        row_max = jnp.max(scores, axis=-1, keepdims=True)
        probs = jnp.exp2(scores * factor - row_max * factor)
        total = jnp.sum(probs, axis=-1, keepdims=True)
        mixed = jnp.dot(probs.astype(jnp.bfloat16), value, preferred_element_type=jnp.float32)
        mixed = (mixed / total).astype(jnp.bfloat16)
        old = latent[start : start + chunk]
        drift = rate * mixed.astype(jnp.float32)
        drift = drift + jnp.where(time == 0, old.astype(jnp.float32), 0.0)
        drift = drift.astype(jnp.bfloat16)
        for target in range(across):
            earlier = jnp.where(target < own_x, old, mixed)
            sent_ref[target, start : start + chunk, :] = jnp.where(target > own_x, drift, earlier)


def gather_kernel(times_ref, modulation_ref, own_ref, along_ref, upto_ref, given_ref):
    across, heads, rows, size = along_ref.shape
    own_x, odd, time = lax.axis_index(ACROSS), lax.axis_index("core") == 1, own_time()
    later = jnp.minimum(own_x + 1, across - 1)
    step = step_size(times_ref, time)
    for head in range(heads):
        columns = slice(head * size, (head + 1) * size)
        own = own_ref[:, columns]
        earlier = jnp.zeros((rows, size), jnp.float32)
        for source in range(across - 1):
            term = along_ref[source, head].astype(jnp.float32)
            earlier = earlier + jnp.where(source < own_x, term, 0.0)
        drift = (step * modulation_ref[2, :, columns]) * along_ref[own_x, head].astype(jnp.float32)
        first = jnp.where(time == 0, own.astype(jnp.float32), 0.0)
        upto = earlier + (drift + first)
        upto_ref[:, columns] = upto
        given_ref[:rows, columns] = jnp.where(odd, earlier, upto).astype(jnp.bfloat16)
        given_ref[rows:, columns] = jnp.where(odd, own, along_ref[later, head])


def finish_kernel(upto_ref, pairs_ref, end_ref, new_ref, error_ref):
    rows, width = upto_ref.shape
    odd = lax.axis_index("core") == 1
    last = jnp.logical_and(odd, lax.axis_index(ACROSS) == lax.axis_size(ACROSS) - 1)
    squares = jnp.zeros((rows, 128), jnp.float32)
    for start in range(0, width, 512):
        columns = slice(start, start + 512)
        other = jnp.where(odd, pairs_ref[0, :, columns], pairs_ref[1, :, columns])
        updated = upto_ref[:, columns] + other[:rows].astype(jnp.float32)
        new_ref[:, columns] = updated.astype(jnp.bfloat16)
        old = jnp.where(last, end_ref[:, columns], other[rows:])
        change = updated - old.astype(jnp.float32)
        change = change * change
        for part in range(0, 512, 128):
            squares = squares + change[:, part : part + 128]
    error_ref[...] = jnp.sum(squares.T, axis=0, keepdims=True) * (1.0 / width)


def body(latents, end_latent, timesteps, modulation, proj_weight):
    heads, size = proj_weight.shape[1], proj_weight.shape[2]
    rows, width = latents.shape[1:]
    across, group = lax.axis_size(ACROSS), lax.axis_size(ORDER)
    copies = group // heads

    def low(*shape):
        return jax.ShapeDtypeStruct(shape, jnp.bfloat16)

    def wide(*shape):
        return jax.ShapeDtypeStruct(shape, jnp.float32)

    inputs = (
        latents[0],
        proj_weight,
        modulation.transpose(1, 0, 2),
        timesteps.reshape(1, -1),
        end_latent,
    )
    sent, own_latent, weights, modulation, timesteps, end_latent = call(
        cut_kernel,
        [
            low(heads // AFTER, copies, AFTER, rows, size),
            low(rows, width),
            low(3, size, size),
            wide(3, 1, width),
            jax.ShapeDtypeStruct((1, timesteps.shape[0]), jnp.int32),
            low(rows, width),
        ],
        *(pltpu.with_memory_space_constraint(operand, pltpu.HBM) for operand in inputs),
        specs=[HBM] * len(inputs),
        scratch=[pltpu.SemaphoreType.DMA] * len(inputs),
    )
    tokens = lax.all_to_all(sent.reshape(group, rows, size), ORDER, 0, 0, tiled=True)
    sent = call(
        functools.partial(attend_kernel, 256),
        low(across, heads * rows, size),
        tokens.reshape(heads // AFTER, copies, AFTER * rows, size),
        timesteps,
        modulation,
        weights,
    )
    along = lax.all_to_all(
        sent.reshape(across * heads, rows, size), ACROSS + NEAR, 0, 0, tiled=True
    )
    upto, given = call(
        gather_kernel,
        [wide(rows, width), low(2 * rows, width)],
        timesteps,
        modulation,
        own_latent,
        along.reshape(across, heads, rows, size),
    )
    pairs = lax.all_gather(given, "core")
    new, error = call(finish_kernel, [low(rows, width), wide(1, rows)], upto, pairs, end_latent)
    return (new[None], error)


def solution(mesh):
    names = ACROSS + ("core",) + BITS
    inner = Mesh(mesh.devices.reshape((2,) * len(names)), names)
    time = ACROSS + ("core",)
    return jax.shard_map(
        body,
        mesh=inner,
        in_specs=(P(time, BITS, None), P(BITS, None), P(), P(time, None, None), P()),
        out_specs=(P(time, BITS, None), P(time, BITS)),
        check_vma=False,
    )
```

```python
import functools
import math

import jax
import jax.numpy as jnp
from jax import lax
from jax.experimental import pallas as pl
from jax.experimental.pallas import tpu as pltpu
from jax.sharding import Mesh, PartitionSpec as P

VMEM = pl.BlockSpec(memory_space=pltpu.VMEM)
HBM = pl.BlockSpec(memory_space=pltpu.HBM)


def call(kernel, shapes, *operands, specs=None, scratch=()):
    return pl.pallas_call(
        kernel,
        out_shape=shapes,
        in_specs=[VMEM] * len(operands) if specs is None else specs,
        out_specs=jax.tree.map(lambda _: VMEM, shapes),
        scratch_shapes=scratch,
        compiler_params=pltpu.CompilerParams(vmem_limit_bytes=32 << 20),
    )(*operands)


BITS = ("y2", "y1", "y0", "z2", "z1", "z0")
ORDER = ('y0', 'y1', 'y2', 'z2', 'z1', 'z0')
FAR = "z2"
NEAR = tuple(axis for axis in ORDER if axis != FAR)
ACROSS = ("x1", "x0")
AFTER = 1 << (len(ORDER) - 1 - ORDER.index(FAR))


def step_size(times_ref, time):
    times = times_ref[...].astype(jnp.float32) / 1000.0
    sigmas = 5.0 * times / (1.0 + 4.0 * times)
    points = lax.broadcasted_iota(jnp.int32, sigmas.shape, 1)
    signed = jnp.where(points == time + 1, sigmas, jnp.where(points == time, -sigmas, 0.0))
    return jnp.sum(signed, axis=-1, keepdims=True)


def own_time():
    return lax.axis_index(ACROSS) * lax.axis_size("core") + lax.axis_index("core")


def cut_kernel(
    latent_hbm, weights_hbm, modulation_hbm, times_hbm, end_hbm,
    sent_ref, own_ref, weights_ref, modulation_ref, times_ref, end_ref,
    *done,
):
    before, copies, after, _, size = sent_ref.shape
    fetches = [
        pltpu.make_async_copy(source, target, semaphore)
        for source, target, semaphore in (
            (latent_hbm, own_ref, done[0]),
            (weights_hbm.at[:, lax.axis_index(NEAR)], weights_ref, done[1]),
            (modulation_hbm, modulation_ref, done[2]),
            (times_hbm, times_ref, done[3]),
            (end_hbm, end_ref, done[4]),
        )
    ]
    for fetch in fetches:
        fetch.start()
    fetches[0].wait()
    for head in range(before * after):
        block = own_ref[:, head * size : (head + 1) * size]
        for copy in range(copies):
            sent_ref[head // after, copy, head % after] = block
    for fetch in fetches[1:]:
        fetch.wait()


def attend_kernel(chunk, tokens_ref, times_ref, modulation_ref, weights_ref, sent_ref):
    heads, across, rows, size = sent_ref.shape
    queries = heads * rows
    columns = pl.ds(pl.multiple_of(lax.axis_index(NEAR) * size, size), size)
    own_x, time = lax.axis_index(ACROSS), own_time()
    shift, scale = modulation_ref[0, :, columns], modulation_ref[1, :, columns]
    rate = step_size(times_ref, time) * modulation_ref[2, :, columns]

    def modulate(block):
        return (block.astype(jnp.float32) * (1.0 + scale) + shift).astype(jnp.bfloat16)

    def project(block, which):
        product = jnp.dot(block, weights_ref[which], preferred_element_type=jnp.float32)
        return product.astype(jnp.bfloat16)

    every = modulate(tokens_ref[...].reshape(2 * queries, size))
    latent = tokens_ref[:, lax.axis_index(FAR)].reshape(queries, size)
    query, key, value = project(modulate(latent), 0), project(every, 1), project(every, 2)
    factor = math.log2(math.e) / math.sqrt(size)

    def score(start):
        block = query[start : start + chunk]
        return lax.dot_general(
            block, key, (((1,), (1,)), ((), ())), preferred_element_type=jnp.float32
        )

    following = score(0)
    for start in range(0, queries, chunk):
        scores = following
        if start + chunk < queries:
            following = score(start + chunk)
        row_max = jnp.max(scores, axis=-1, keepdims=True)
        probs = jnp.exp2((scores - row_max) * factor)
        total = jnp.sum(probs, axis=-1, keepdims=True)
        mixed = jnp.dot(probs.astype(jnp.bfloat16), value, preferred_element_type=jnp.float32)
        mixed = (mixed / total).astype(jnp.bfloat16)
        old = latent[start : start + chunk]
        drift = rate * mixed.astype(jnp.float32)
        drift = drift + jnp.where(time == 0, old.astype(jnp.float32), 0.0)
        drift = drift.astype(jnp.bfloat16)
        for target in range(across):
            earlier = jnp.where(target < own_x, old, mixed)
            block = jnp.where(target > own_x, drift, earlier)
            sent_ref[start // rows : (start + chunk) // rows, target] = block.reshape(chunk // rows, rows, size)


def gather_kernel(times_ref, modulation_ref, own_ref, along_ref, upto_ref, given_ref):
    heads, across, rows, size = along_ref.shape
    own_x, odd, time = lax.axis_index(ACROSS), lax.axis_index("core") == 1, own_time()
    later = jnp.minimum(own_x + 1, across - 1)
    step = step_size(times_ref, time)
    for head in range(heads):
        columns = slice(head * size, (head + 1) * size)
        own = own_ref[:, columns]
        earlier = jnp.zeros((rows, size), jnp.float32)
        for source in range(across - 1):
            term = along_ref[head, source].astype(jnp.float32)
            earlier = earlier + jnp.where(source < own_x, term, 0.0)
        drift = (step * modulation_ref[2, :, columns]) * along_ref[head, own_x].astype(jnp.float32)
        first = jnp.where(time == 0, own.astype(jnp.float32), 0.0)
        upto = earlier + (drift + first)
        upto_ref[:, columns] = upto
        given_ref[:rows, columns] = jnp.where(odd, earlier, upto).astype(jnp.bfloat16)
        given_ref[rows:, columns] = jnp.where(odd, own, along_ref[head, later])


def finish_kernel(upto_ref, pairs_ref, end_ref, new_ref, error_ref):
    rows, width = upto_ref.shape
    odd = lax.axis_index("core") == 1
    last = jnp.logical_and(odd, lax.axis_index(ACROSS) == lax.axis_size(ACROSS) - 1)
    squares = jnp.zeros((rows, 128), jnp.float32)
    for start in range(0, width, 512):
        columns = slice(start, start + 512)
        other = jnp.where(odd, pairs_ref[0, :, columns], pairs_ref[1, :, columns])
        updated = upto_ref[:, columns] + other[:rows].astype(jnp.float32)
        new_ref[:, columns] = updated.astype(jnp.bfloat16)
        old = jnp.where(last, end_ref[:, columns], other[rows:])
        change = updated - old.astype(jnp.float32)
        change = change * change
        for part in range(0, 512, 128):
            squares = squares + change[:, part : part + 128]
    error_ref[...] = jnp.sum(squares.T, axis=0, keepdims=True) * (1.0 / width)


def body(latents, end_latent, timesteps, modulation, proj_weight):
    heads, size = proj_weight.shape[1], proj_weight.shape[2]
    rows, width = latents.shape[1:]
    across, group = lax.axis_size(ACROSS), lax.axis_size(ORDER)
    copies = group // heads

    def low(*shape):
        return jax.ShapeDtypeStruct(shape, jnp.bfloat16)

    def wide(*shape):
        return jax.ShapeDtypeStruct(shape, jnp.float32)

    inputs = (
        latents[0],
        proj_weight,
        modulation.transpose(1, 0, 2),
        timesteps.reshape(1, -1),
        end_latent,
    )
    sent, own_latent, weights, modulation, timesteps, end_latent = call(
        cut_kernel,
        [
            low(heads // AFTER, copies, AFTER, rows, size),
            low(rows, width),
            low(3, size, size),
            wide(3, 1, width),
            jax.ShapeDtypeStruct((1, timesteps.shape[0]), jnp.int32),
            low(rows, width),
        ],
        *(pltpu.with_memory_space_constraint(operand, pltpu.HBM) for operand in inputs),
        specs=[HBM] * len(inputs),
        scratch=[pltpu.SemaphoreType.DMA] * len(inputs),
    )
    tokens = lax.all_to_all(sent.reshape(group, rows, size), ORDER, 0, 0, tiled=True)
    sent = call(
        functools.partial(attend_kernel, 256),
        low(heads, across, rows, size),
        tokens.reshape(heads // AFTER, copies, AFTER * rows, size),
        timesteps,
        modulation,
        weights,
    )
    along = lax.all_to_all(
        sent.reshape(across * heads, rows, size), NEAR + ACROSS, 0, 0, tiled=True
    )
    upto, given = call(
        gather_kernel,
        [wide(rows, width), low(2 * rows, width)],
        timesteps,
        modulation,
        own_latent,
        along.reshape(heads, across, rows, size),
    )
    pairs = lax.all_gather(given, "core")
    new, error = call(finish_kernel, [low(rows, width), wide(1, rows)], upto, pairs, end_latent)
    return (new[None], error)


def solution(mesh):
    names = ACROSS + ("core",) + BITS
    inner = Mesh(mesh.devices.reshape((2,) * len(names)), names)
    time = ACROSS + ("core",)
    return jax.shard_map(
        body,
        mesh=inner,
        in_specs=(P(time, BITS, None), P(BITS, None), P(), P(time, None, None), P()),
        out_specs=(P(time, BITS, None), P(time, BITS)),
        check_vma=False,
    )
```

```python
import functools
import math

import jax
import jax.numpy as jnp
from jax import lax
from jax.experimental import pallas as pl
from jax.experimental.pallas import tpu as pltpu
from jax.sharding import Mesh, PartitionSpec as P

VMEM = pl.BlockSpec(memory_space=pltpu.VMEM)
HBM = pl.BlockSpec(memory_space=pltpu.HBM)


def call(kernel, shapes, *operands, specs=None, scratch=()):
    return pl.pallas_call(
        kernel,
        out_shape=shapes,
        in_specs=[VMEM] * len(operands) if specs is None else specs,
        out_specs=jax.tree.map(lambda _: VMEM, shapes),
        scratch_shapes=scratch,
        compiler_params=pltpu.CompilerParams(vmem_limit_bytes=32 << 20),
    )(*operands)


BITS = ("y2", "y1", "y0", "z2", "z1", "z0")
ORDER = ("z2", "y0", "y2", "y1", "z1", "z0")
FAR = "z2"
NEAR = tuple(axis for axis in ORDER if axis != FAR)
ACROSS = ("x1", "x0")
AFTER = 1 << (len(ORDER) - 1 - ORDER.index(FAR))


def step_size(times_ref, time):
    times = times_ref[...].astype(jnp.float32) / 1000.0
    sigmas = 5.0 * times / (1.0 + 4.0 * times)
    points = lax.broadcasted_iota(jnp.int32, sigmas.shape, 1)
    signed = jnp.where(points == time + 1, sigmas, jnp.where(points == time, -sigmas, 0.0))
    return jnp.sum(signed, axis=-1, keepdims=True)


def own_time():
    return lax.axis_index(ACROSS) * lax.axis_size("core") + lax.axis_index("core")


def cut_kernel(
    latent_hbm, weights_hbm, modulation_hbm, times_hbm, end_hbm,
    sent_ref, own_ref, weights_ref, modulation_ref, times_ref, end_ref,
    *done,
):
    before, copies, after, _, size = sent_ref.shape
    fetches = [
        pltpu.make_async_copy(source, target, semaphore)
        for source, target, semaphore in (
            (latent_hbm, own_ref, done[0]),
            (weights_hbm.at[:, lax.axis_index(NEAR)], weights_ref, done[1]),
            (modulation_hbm, modulation_ref, done[2]),
            (times_hbm, times_ref, done[3]),
            (end_hbm, end_ref, done[4]),
        )
    ]
    for fetch in fetches:
        fetch.start()
    fetches[0].wait()
    for head in range(before * after):
        block = own_ref[:, head * size : (head + 1) * size]
        for copy in range(copies):
            sent_ref[head // after, copy, head % after] = block
    for fetch in fetches[1:]:
        fetch.wait()


def attend_kernel(chunk, tokens_ref, times_ref, modulation_ref, weights_ref, sent_ref):
    heads, across, rows, size = sent_ref.shape
    queries = heads * rows
    columns = pl.ds(pl.multiple_of(lax.axis_index(NEAR) * size, size), size)
    own_x, time = lax.axis_index(ACROSS), own_time()
    shift, scale = modulation_ref[0, :, columns], modulation_ref[1, :, columns]
    rate = step_size(times_ref, time) * modulation_ref[2, :, columns]

    def modulate(block):
        return (block.astype(jnp.float32) * (1.0 + scale) + shift).astype(jnp.bfloat16)

    def project(block, which):
        product = jnp.dot(block, weights_ref[which], preferred_element_type=jnp.float32)
        return product.astype(jnp.bfloat16)

    every = modulate(tokens_ref[...].reshape(2 * queries, size))
    latent = tokens_ref[:, lax.axis_index(FAR)].reshape(queries, size)
    query, key, value = project(modulate(latent), 0), project(every, 1), project(every, 2)
    factor = math.log2(math.e) / math.sqrt(size)

    def score(start):
        block = query[start : start + chunk]
        return lax.dot_general(
            block, key, (((1,), (1,)), ((), ())), preferred_element_type=jnp.float32
        )

    following = score(0)
    for start in range(0, queries, chunk):
        scores = following
        if start + chunk < queries:
            following = score(start + chunk)
        row_max = jnp.max(scores, axis=-1, keepdims=True)
        probs = jnp.exp2((scores - row_max) * factor)
        total = jnp.sum(probs, axis=-1, keepdims=True)
        mixed = jnp.dot(probs.astype(jnp.bfloat16), value, preferred_element_type=jnp.float32)
        mixed = (mixed / total).astype(jnp.bfloat16)
        old = latent[start : start + chunk]
        drift = rate * mixed.astype(jnp.float32)
        drift = drift + jnp.where(time == 0, old.astype(jnp.float32), 0.0)
        drift = drift.astype(jnp.bfloat16)
        for target in range(across):
            earlier = jnp.where(target < own_x, old, mixed)
            block = jnp.where(target > own_x, drift, earlier)
            sent_ref[start // rows : (start + chunk) // rows, target] = block.reshape(chunk // rows, rows, size)


def gather_kernel(times_ref, modulation_ref, own_ref, along_ref, upto_ref, given_ref):
    heads, across, rows, size = along_ref.shape
    own_x, odd, time = lax.axis_index(ACROSS), lax.axis_index("core") == 1, own_time()
    later = jnp.minimum(own_x + 1, across - 1)
    step = step_size(times_ref, time)
    for head in range(heads):
        columns = slice(head * size, (head + 1) * size)
        own = own_ref[:, columns]
        earlier = jnp.zeros((rows, size), jnp.float32)
        for source in range(across - 1):
            term = along_ref[head, source].astype(jnp.float32)
            earlier = earlier + jnp.where(source < own_x, term, 0.0)
        drift = (step * modulation_ref[2, :, columns]) * along_ref[head, own_x].astype(jnp.float32)
        first = jnp.where(time == 0, own.astype(jnp.float32), 0.0)
        upto = earlier + (drift + first)
        upto_ref[:, columns] = upto
        given_ref[:rows, columns] = jnp.where(odd, earlier, upto).astype(jnp.bfloat16)
        given_ref[rows:, columns] = jnp.where(odd, own, along_ref[head, later])


def finish_kernel(upto_ref, pairs_ref, end_ref, new_ref, error_ref):
    rows, width = upto_ref.shape
    odd = lax.axis_index("core") == 1
    last = jnp.logical_and(odd, lax.axis_index(ACROSS) == lax.axis_size(ACROSS) - 1)
    squares = jnp.zeros((rows, 128), jnp.float32)
    for start in range(0, width, 512):
        columns = slice(start, start + 512)
        other = jnp.where(odd, pairs_ref[0, :, columns], pairs_ref[1, :, columns])
        updated = upto_ref[:, columns] + other[:rows].astype(jnp.float32)
        new_ref[:, columns] = updated.astype(jnp.bfloat16)
        old = jnp.where(last, end_ref[:, columns], other[rows:])
        change = updated - old.astype(jnp.float32)
        change = change * change
        for part in range(0, 512, 128):
            squares = squares + change[:, part : part + 128]
    error_ref[...] = jnp.sum(squares.T, axis=0, keepdims=True) * (1.0 / width)


def body(latents, end_latent, timesteps, modulation, proj_weight):
    heads, size = proj_weight.shape[1], proj_weight.shape[2]
    rows, width = latents.shape[1:]
    across, group = lax.axis_size(ACROSS), lax.axis_size(ORDER)
    copies = group // heads

    def low(*shape):
        return jax.ShapeDtypeStruct(shape, jnp.bfloat16)

    def wide(*shape):
        return jax.ShapeDtypeStruct(shape, jnp.float32)

    inputs = (
        latents[0],
        proj_weight,
        modulation.transpose(1, 0, 2),
        timesteps.reshape(1, -1),
        end_latent,
    )
    sent, own_latent, weights, modulation, timesteps, end_latent = call(
        cut_kernel,
        [
            low(heads // AFTER, copies, AFTER, rows, size),
            low(rows, width),
            low(3, size, size),
            wide(3, 1, width),
            jax.ShapeDtypeStruct((1, timesteps.shape[0]), jnp.int32),
            low(rows, width),
        ],
        *(pltpu.with_memory_space_constraint(operand, pltpu.HBM) for operand in inputs),
        specs=[HBM] * len(inputs),
        scratch=[pltpu.SemaphoreType.DMA] * len(inputs),
    )
    tokens = lax.all_to_all(sent.reshape(group, rows, size), ORDER, 0, 0, tiled=True)
    sent = call(
        functools.partial(attend_kernel, 256),
        low(heads, across, rows, size),
        tokens.reshape(heads // AFTER, copies, AFTER * rows, size),
        timesteps,
        modulation,
        weights,
    )
    along = lax.all_to_all(
        sent.reshape(across * heads, rows, size), NEAR + ACROSS, 0, 0, tiled=True
    )
    upto, given = call(
        gather_kernel,
        [wide(rows, width), low(2 * rows, width)],
        timesteps,
        modulation,
        own_latent,
        along.reshape(heads, across, rows, size),
    )
    pairs = lax.all_gather(given, "core")
    new, error = call(finish_kernel, [low(rows, width), wide(1, rows)], upto, pairs, end_latent)
    return (new[None], error)


def solution(mesh):
    names = ACROSS + ("core",) + BITS
    inner = Mesh(mesh.devices.reshape((2,) * len(names)), names)
    time = ACROSS + ("core",)
    return jax.shard_map(
        body,
        mesh=inner,
        in_specs=(P(time, BITS, None), P(BITS, None), P(), P(time, None, None), P()),
        out_specs=(P(time, BITS, None), P(time, BITS)),
        check_vma=False,
    )
```

```python
import functools
import math

import jax
import jax.numpy as jnp
from jax import lax
from jax.experimental import pallas as pl
from jax.experimental.pallas import tpu as pltpu
from jax.sharding import Mesh, PartitionSpec as P

VMEM = pl.BlockSpec(memory_space=pltpu.VMEM)
HBM = pl.BlockSpec(memory_space=pltpu.HBM)


def call(kernel, shapes, *operands, specs=None, scratch=()):
    return pl.pallas_call(
        kernel,
        out_shape=shapes,
        in_specs=[VMEM] * len(operands) if specs is None else specs,
        out_specs=jax.tree.map(lambda _: VMEM, shapes),
        scratch_shapes=scratch,
        compiler_params=pltpu.CompilerParams(vmem_limit_bytes=32 << 20),
    )(*operands)


BITS = ("y2", "y1", "y0", "z2", "z1", "z0")
ORDER = ("z2", "y0", "y2", "y1", "z1", "z0")
FAR = "z2"
NEAR = tuple(axis for axis in ORDER if axis != FAR)
ACROSS = ("x1", "x0")
AFTER = 1 << (len(ORDER) - 1 - ORDER.index(FAR))


def step_size(times_ref, time):
    times = times_ref[...].astype(jnp.float32) / 1000.0
    sigmas = 5.0 * times / (1.0 + 4.0 * times)
    points = lax.broadcasted_iota(jnp.int32, sigmas.shape, 1)
    signed = jnp.where(points == time + 1, sigmas, jnp.where(points == time, -sigmas, 0.0))
    return jnp.sum(signed, axis=-1, keepdims=True)


def own_time():
    return lax.axis_index(ACROSS) * lax.axis_size("core") + lax.axis_index("core")


def cut_kernel(
    latent_hbm, weights_hbm, modulation_hbm, times_hbm, end_hbm,
    sent_ref, own_ref, weights_ref, modulation_ref, times_ref, end_ref,
    *done,
):
    before, copies, after, _, size = sent_ref.shape
    fetches = [
        pltpu.make_async_copy(source, target, semaphore)
        for source, target, semaphore in (
            (latent_hbm, own_ref, done[0]),
            (weights_hbm.at[:, lax.axis_index(NEAR)], weights_ref, done[1]),
            (modulation_hbm, modulation_ref, done[2]),
            (times_hbm, times_ref, done[3]),
            (end_hbm, end_ref, done[4]),
        )
    ]
    for fetch in fetches:
        fetch.start()
    fetches[0].wait()
    for head in range(before * after):
        block = own_ref[:, head * size : (head + 1) * size]
        for copy in range(copies):
            sent_ref[head // after, copy, head % after] = block
    for fetch in fetches[1:]:
        fetch.wait()


def attend_kernel(chunk, tokens_ref, times_ref, modulation_ref, weights_ref, sent_ref):
    outer, across, inner, rows, size = sent_ref.shape
    queries = outer * inner * rows
    step = inner * rows
    columns = pl.ds(pl.multiple_of(lax.axis_index(NEAR) * size, size), size)
    own_x, time = lax.axis_index(ACROSS), own_time()
    shift, scale = modulation_ref[0, :, columns], modulation_ref[1, :, columns]
    rate = step_size(times_ref, time) * modulation_ref[2, :, columns]

    def modulate(block):
        return (block.astype(jnp.float32) * (1.0 + scale) + shift).astype(jnp.bfloat16)

    def project(block, which):
        product = jnp.dot(block, weights_ref[which], preferred_element_type=jnp.float32)
        return product.astype(jnp.bfloat16)

    every = modulate(tokens_ref[...].reshape(2 * queries, size))
    latent = tokens_ref[:, lax.axis_index(FAR)].reshape(queries, size)
    query, key, value = project(modulate(latent), 0), project(every, 1), project(every, 2)
    factor = math.log2(math.e) / math.sqrt(size)

    def score(start):
        block = query[start : start + chunk]
        return lax.dot_general(
            block, key, (((1,), (1,)), ((), ())), preferred_element_type=jnp.float32
        )

    following = score(0)
    for start in range(0, queries, chunk):
        scores = following
        if start + chunk < queries:
            following = score(start + chunk)
        row_max = jnp.max(scores, axis=-1, keepdims=True)
        probs = jnp.exp2((scores - row_max) * factor)
        total = jnp.sum(probs, axis=-1, keepdims=True)
        mixed = jnp.dot(probs.astype(jnp.bfloat16), value, preferred_element_type=jnp.float32)
        mixed = (mixed / total).astype(jnp.bfloat16)
        old = latent[start : start + chunk]
        drift = rate * mixed.astype(jnp.float32)
        drift = drift + jnp.where(time == 0, old.astype(jnp.float32), 0.0)
        drift = drift.astype(jnp.bfloat16)
        for target in range(across):
            earlier = jnp.where(target < own_x, old, mixed)
            block = jnp.where(target > own_x, drift, earlier)
            sent_ref[start // step : (start + chunk) // step, target] = block.reshape(
                chunk // step, inner, rows, size
            )


def gather_kernel(times_ref, modulation_ref, own_ref, along_ref, upto_ref, given_ref):
    outer, across, inner, rows, size = along_ref.shape
    heads = outer * inner
    own_x, odd, time = lax.axis_index(ACROSS), lax.axis_index("core") == 1, own_time()
    later = jnp.minimum(own_x + 1, across - 1)
    step = step_size(times_ref, time)
    for head in range(heads):
        columns = slice(head * size, (head + 1) * size)
        own = own_ref[:, columns]
        earlier = jnp.zeros((rows, size), jnp.float32)
        for source in range(across - 1):
            term = along_ref[head // inner, source, head % inner].astype(jnp.float32)
            earlier = earlier + jnp.where(source < own_x, term, 0.0)
        drift = (step * modulation_ref[2, :, columns]) * along_ref[head // inner, own_x, head % inner].astype(jnp.float32)
        first = jnp.where(time == 0, own.astype(jnp.float32), 0.0)
        upto = earlier + (drift + first)
        upto_ref[:, columns] = upto
        given_ref[:rows, columns] = jnp.where(odd, earlier, upto).astype(jnp.bfloat16)
        given_ref[rows:, columns] = jnp.where(odd, own, along_ref[head // inner, later, head % inner])


def finish_kernel(upto_ref, pairs_ref, end_ref, new_ref, error_ref):
    rows, width = upto_ref.shape
    odd = lax.axis_index("core") == 1
    last = jnp.logical_and(odd, lax.axis_index(ACROSS) == lax.axis_size(ACROSS) - 1)
    squares = jnp.zeros((rows, 128), jnp.float32)
    for start in range(0, width, 512):
        columns = slice(start, start + 512)
        other = jnp.where(odd, pairs_ref[0, :, columns], pairs_ref[1, :, columns])
        updated = upto_ref[:, columns] + other[:rows].astype(jnp.float32)
        new_ref[:, columns] = updated.astype(jnp.bfloat16)
        old = jnp.where(last, end_ref[:, columns], other[rows:])
        change = updated - old.astype(jnp.float32)
        change = change * change
        for part in range(0, 512, 128):
            squares = squares + change[:, part : part + 128]
    error_ref[...] = jnp.sum(squares.T, axis=0, keepdims=True) * (1.0 / width)


def body(latents, end_latent, timesteps, modulation, proj_weight):
    heads, size = proj_weight.shape[1], proj_weight.shape[2]
    rows, width = latents.shape[1:]
    across, group = lax.axis_size(ACROSS), lax.axis_size(ORDER)
    copies = group // heads

    def low(*shape):
        return jax.ShapeDtypeStruct(shape, jnp.bfloat16)

    def wide(*shape):
        return jax.ShapeDtypeStruct(shape, jnp.float32)

    inputs = (
        latents[0],
        proj_weight,
        modulation.transpose(1, 0, 2),
        timesteps.reshape(1, -1),
        end_latent,
    )
    sent, own_latent, weights, modulation, timesteps, end_latent = call(
        cut_kernel,
        [
            low(heads // AFTER, copies, AFTER, rows, size),
            low(rows, width),
            low(3, size, size),
            wide(3, 1, width),
            jax.ShapeDtypeStruct((1, timesteps.shape[0]), jnp.int32),
            low(rows, width),
        ],
        *(pltpu.with_memory_space_constraint(operand, pltpu.HBM) for operand in inputs),
        specs=[HBM] * len(inputs),
        scratch=[pltpu.SemaphoreType.DMA] * len(inputs),
    )
    tokens = lax.all_to_all(sent.reshape(group, rows, size), ORDER, 0, 0, tiled=True)
    sent = call(
        functools.partial(attend_kernel, 256),
        low(heads // 4, across, 4, rows, size),
        tokens.reshape(heads // AFTER, copies, AFTER * rows, size),
        timesteps,
        modulation,
        weights,
    )
    along = lax.all_to_all(
        sent.reshape(across * heads, rows, size), NEAR[:3] + ACROSS + NEAR[3:], 0, 0, tiled=True
    )
    upto, given = call(
        gather_kernel,
        [wide(rows, width), low(2 * rows, width)],
        timesteps,
        modulation,
        own_latent,
        along.reshape(heads // 4, across, 4, rows, size),
    )
    pairs = lax.all_gather(given, "core")
    new, error = call(finish_kernel, [low(rows, width), wide(1, rows)], upto, pairs, end_latent)
    return (new[None], error)


def solution(mesh):
    names = ACROSS + ("core",) + BITS
    inner = Mesh(mesh.devices.reshape((2,) * len(names)), names)
    time = ACROSS + ("core",)
    return jax.shard_map(
        body,
        mesh=inner,
        in_specs=(P(time, BITS, None), P(BITS, None), P(), P(time, None, None), P()),
        out_specs=(P(time, BITS, None), P(time, BITS)),
        check_vma=False,
    )
```

```python
import functools
import math

import jax
import jax.numpy as jnp
from jax import lax
from jax.experimental import pallas as pl
from jax.experimental.pallas import tpu as pltpu
from jax.sharding import Mesh, PartitionSpec as P

VMEM = pl.BlockSpec(memory_space=pltpu.VMEM)
HBM = pl.BlockSpec(memory_space=pltpu.HBM)


def call(kernel, shapes, *operands, specs=None, scratch=()):
    return pl.pallas_call(
        kernel,
        out_shape=shapes,
        in_specs=[VMEM] * len(operands) if specs is None else specs,
        out_specs=jax.tree.map(lambda _: VMEM, shapes),
        scratch_shapes=scratch,
        compiler_params=pltpu.CompilerParams(vmem_limit_bytes=32 << 20),
    )(*operands)


BITS = ("y2", "y1", "y0", "z2", "z1", "z0")
ORDER = ("z2", "y0", "y2", "y1", "z1", "z0")
FAR = "z2"
NEAR = tuple(axis for axis in ORDER if axis != FAR)
ACROSS = ("x1", "x0")
AFTER = 1 << (len(ORDER) - 1 - ORDER.index(FAR))


def step_size(times_ref, time):
    times = times_ref[...].astype(jnp.float32) / 1000.0
    sigmas = 5.0 * times / (1.0 + 4.0 * times)
    points = lax.broadcasted_iota(jnp.int32, sigmas.shape, 1)
    signed = jnp.where(points == time + 1, sigmas, jnp.where(points == time, -sigmas, 0.0))
    return jnp.sum(signed, axis=-1, keepdims=True)


def own_time():
    return lax.axis_index(ACROSS) * lax.axis_size("core") + lax.axis_index("core")


def cut_kernel(
    latent_hbm, weights_hbm, modulation_hbm, times_hbm, end_hbm,
    sent_ref, own_ref, weights_ref, modulation_ref, times_ref, end_ref,
    *done,
):
    before, copies, after, _, size = sent_ref.shape
    width = own_ref.shape[1] // 4
    pieces = [slice(start, start + width) for start in range(0, 4 * width, width)]
    fetches = [
        pltpu.make_async_copy(latent_hbm.at[:, piece], own_ref.at[:, piece], semaphore)
        for piece, semaphore in zip(pieces, done[4:])
    ] + [
        pltpu.make_async_copy(source, target, semaphore)
        for source, target, semaphore in (
            (weights_hbm.at[:, lax.axis_index(NEAR)], weights_ref, done[0]),
            (modulation_hbm, modulation_ref, done[1]),
            (times_hbm, times_ref, done[2]),
            (end_hbm, end_ref, done[3]),
        )
    ]
    for fetch in fetches:
        fetch.start()
    for head in range(before * after):
        if head * size % width == 0:
            fetches[head * size // width].wait()
        block = own_ref[:, head * size : (head + 1) * size]
        for copy in range(copies):
            sent_ref[head // after, copy, head % after] = block
    for fetch in fetches[4:]:
        fetch.wait()


def attend_kernel(chunk, tokens_ref, times_ref, modulation_ref, weights_ref, sent_ref):
    outer, across, inner, rows, size = sent_ref.shape
    queries = outer * inner * rows
    step = inner * rows
    columns = pl.ds(pl.multiple_of(lax.axis_index(NEAR) * size, size), size)
    own_x, time = lax.axis_index(ACROSS), own_time()
    shift, scale = modulation_ref[0, :, columns], modulation_ref[1, :, columns]
    rate = step_size(times_ref, time) * modulation_ref[2, :, columns]

    def modulate(block):
        return (block.astype(jnp.float32) * (1.0 + scale) + shift).astype(jnp.bfloat16)

    def project(block, which):
        product = jnp.dot(block, weights_ref[which], preferred_element_type=jnp.float32)
        return product.astype(jnp.bfloat16)

    every = modulate(tokens_ref[...].reshape(2 * queries, size))
    latent = tokens_ref[:, lax.axis_index(FAR)].reshape(queries, size)
    query, key, value = project(modulate(latent), 0), project(every, 1), project(every, 2)
    factor = math.log2(math.e) / math.sqrt(size)

    def score(start):
        block = query[start : start + chunk]
        return lax.dot_general(
            block, key, (((1,), (1,)), ((), ())), preferred_element_type=jnp.float32
        )

    following = score(0)
    for start in range(0, queries, chunk):
        scores = following
        if start + chunk < queries:
            following = score(start + chunk)
        row_max = jnp.max(scores, axis=-1, keepdims=True)
        probs = jnp.exp2((scores - row_max) * factor)
        total = jnp.sum(probs, axis=-1, keepdims=True)
        mixed = jnp.dot(probs.astype(jnp.bfloat16), value, preferred_element_type=jnp.float32)
        mixed = (mixed / total).astype(jnp.bfloat16)
        old = latent[start : start + chunk]
        drift = rate * mixed.astype(jnp.float32)
        drift = drift + jnp.where(time == 0, old.astype(jnp.float32), 0.0)
        drift = drift.astype(jnp.bfloat16)
        for target in range(across):
            earlier = jnp.where(target < own_x, old, mixed)
            block = jnp.where(target > own_x, drift, earlier)
            sent_ref[start // step : (start + chunk) // step, target] = block.reshape(
                chunk // step, inner, rows, size
            )


def gather_kernel(times_ref, modulation_ref, own_ref, along_ref, upto_ref, given_ref):
    outer, across, inner, rows, size = along_ref.shape
    heads = outer * inner
    own_x, odd, time = lax.axis_index(ACROSS), lax.axis_index("core") == 1, own_time()
    later = jnp.minimum(own_x + 1, across - 1)
    step = step_size(times_ref, time)
    for head in range(heads):
        columns = slice(head * size, (head + 1) * size)
        own = own_ref[:, columns]
        earlier = jnp.zeros((rows, size), jnp.float32)
        for source in range(across - 1):
            term = along_ref[head // inner, source, head % inner].astype(jnp.float32)
            earlier = earlier + jnp.where(source < own_x, term, 0.0)
        drift = (step * modulation_ref[2, :, columns]) * along_ref[head // inner, own_x, head % inner].astype(jnp.float32)
        first = jnp.where(time == 0, own.astype(jnp.float32), 0.0)
        upto = earlier + (drift + first)
        upto_ref[:, columns] = upto
        given_ref[:rows, columns] = jnp.where(odd, earlier, upto).astype(jnp.bfloat16)
        given_ref[rows:, columns] = jnp.where(odd, own, along_ref[head // inner, later, head % inner])


def finish_kernel(upto_ref, pairs_ref, end_ref, new_ref, error_ref):
    rows, width = upto_ref.shape
    odd = lax.axis_index("core") == 1
    last = jnp.logical_and(odd, lax.axis_index(ACROSS) == lax.axis_size(ACROSS) - 1)
    squares = jnp.zeros((rows, 128), jnp.float32)
    for start in range(0, width, 512):
        columns = slice(start, start + 512)
        other = jnp.where(odd, pairs_ref[0, :, columns], pairs_ref[1, :, columns])
        updated = upto_ref[:, columns] + other[:rows].astype(jnp.float32)
        new_ref[:, columns] = updated.astype(jnp.bfloat16)
        old = jnp.where(last, end_ref[:, columns], other[rows:])
        change = updated - old.astype(jnp.float32)
        change = change * change
        for part in range(0, 512, 128):
            squares = squares + change[:, part : part + 128]
    error_ref[...] = jnp.sum(squares.T, axis=0, keepdims=True) * (1.0 / width)


def body(latents, end_latent, timesteps, modulation, proj_weight):
    heads, size = proj_weight.shape[1], proj_weight.shape[2]
    rows, width = latents.shape[1:]
    across, group = lax.axis_size(ACROSS), lax.axis_size(ORDER)
    copies = group // heads

    def low(*shape):
        return jax.ShapeDtypeStruct(shape, jnp.bfloat16)

    def wide(*shape):
        return jax.ShapeDtypeStruct(shape, jnp.float32)

    inputs = (
        latents[0],
        proj_weight,
        modulation.transpose(1, 0, 2),
        timesteps.reshape(1, -1),
        end_latent,
    )
    sent, own_latent, weights, modulation, timesteps, end_latent = call(
        cut_kernel,
        [
            low(heads // AFTER, copies, AFTER, rows, size),
            low(rows, width),
            low(3, size, size),
            wide(3, 1, width),
            jax.ShapeDtypeStruct((1, timesteps.shape[0]), jnp.int32),
            low(rows, width),
        ],
        *(pltpu.with_memory_space_constraint(operand, pltpu.HBM) for operand in inputs),
        specs=[HBM] * len(inputs),
        scratch=[pltpu.SemaphoreType.DMA] * (len(inputs) + 3),
    )
    tokens = lax.all_to_all(sent.reshape(group, rows, size), ORDER, 0, 0, tiled=True)
    sent = call(
        functools.partial(attend_kernel, 256),
        low(heads // 4, across, 4, rows, size),
        tokens.reshape(heads // AFTER, copies, AFTER * rows, size),
        timesteps,
        modulation,
        weights,
    )
    along = lax.all_to_all(
        sent.reshape(across * heads, rows, size), NEAR[:3] + ACROSS + NEAR[3:], 0, 0, tiled=True
    )
    upto, given = call(
        gather_kernel,
        [wide(rows, width), low(2 * rows, width)],
        timesteps,
        modulation,
        own_latent,
        along.reshape(heads // 4, across, 4, rows, size),
    )
    pairs = lax.all_gather(given, "core")
    new, error = call(finish_kernel, [low(rows, width), wide(1, rows)], upto, pairs, end_latent)
    return (new[None], error)


def solution(mesh):
    names = ACROSS + ("core",) + BITS
    inner = Mesh(mesh.devices.reshape((2,) * len(names)), names)
    time = ACROSS + ("core",)
    return jax.shard_map(
        body,
        mesh=inner,
        in_specs=(P(time, BITS, None), P(BITS, None), P(), P(time, None, None), P()),
        out_specs=(P(time, BITS, None), P(time, BITS)),
        check_vma=False,
    )
```
